32 devices in a mesh: groups: 2 (over y), seq: 4 (over z), head: 2 (over x), sub: 2 (over core).
Axes of the slice: x: 2, y: 2, z: 4, core: 2. Of those that a mesh axis runs over, the one named last changes fastest.
Arguments:
- queries: bfloat16 [2048, 2048], P(('groups', 'seq'), ('head', 'sub')), parts along dimension 0, may hold values from -6 to 6
- keys: bfloat16 [2048, 2048], P(('groups', 'seq'), ('head', 'sub')), parts along dimension 0, may hold values from -0.25 to 0.25
- values: bfloat16 [2048, 2048], P(('groups', 'seq'), ('head', 'sub')), parts along dimension 0, may hold values from -0.75 to 0.75
- out_grad: bfloat16 [2048, 2048], P(('groups', 'seq'), ('head', 'sub')), parts along dimension 0, may hold values from -0.75 to 0.75
- ridge: float32 [16], P(('head', 'sub')), may hold values from 0.8 to 2.4
Outputs:
- mesa_out: float32 [2048, 2048], P(('groups', 'seq'), ('head', 'sub')), parts along dimension 0
- query_grad: float32 [2048, 2048], P(('groups', 'seq'), ('head', 'sub')), parts along dimension 0
- key_grad: float32 [2048, 2048], P(('groups', 'seq'), ('head', 'sub')), parts along dimension 0
- value_grad: float32 [2048, 2048], P(('groups', 'seq'), ('head', 'sub')), parts along dimension 0
The draws below stay inside these ranges and needn't reach their ends.
There are 2 independent parts, one for each index of `groups`. The reference program is written for one: setup_inputs(seed, part) draws one part's arguments, and reference() takes and returns one part's arrays. A program takes and returns all parts, laid end to end along the dimension named above; an argument that names none is the same for every part. Nothing has to cross between parts.
All inputs are finite; a program needn't handle non-finite values.
Results may differ from the reference program's by a relative error of at most 0.0003.
Values sent between devices are 32-bit elements; how exact they have to be, the bound alone decides.
A program may use at most 64 MiB of HBM per device.

```python
import math
import jax
import jax.numpy as jnp
from jax import lax

HEADS = 16
HEAD_DIM = 128
BLOCK = 128
CG_STEPS = 4
SEQLEN = 1024


def draw_keys(key, part):
    width = HEADS * HEAD_DIM
    spread = jnp.exp(jax.random.uniform(jax.random.fold_in(key, 11), (width,), jnp.float32, jnp.log(0.05), jnp.log(4.0)))
    base = jnp.clip(jax.random.normal(jax.random.fold_in(key, 12), (SEQLEN, width), jnp.float32), -4.0, 4.0)
    scaled = base * jnp.sqrt(spread / SEQLEN)[None, :]
    return scaled.astype(jnp.bfloat16)


def block_scale(rng, shape, shards, smallest, top_value):
    level, own = 1.0, jax.random.fold_in(rng, 6)
    for axis_at, blocks in shards:
        heights = jnp.exp(jax.random.uniform(jax.random.fold_in(own, axis_at), (blocks,), jnp.float32, smallest / len(shards), top_value / len(shards)))
        level = level * jnp.repeat(heights, shape[axis_at] // blocks).reshape([-1 if axis == axis_at else 1 for axis in range(len(shape))])
    return level


def centred(key, extent, scale, limit, shards=(), kind=jnp.bfloat16):
    entries = jax.random.normal(key, extent, jnp.float32) * scale
    if len(shards) > 0:
        entries = block_scale(key, extent, shards, -0.22, 0.18) * entries
    return jnp.clip(entries, min=-limit, max=limit).astype(kind)


def setup_inputs(seed: int = 0, part: int = 0) -> dict:
    splits = jax.random.split(jax.random.key(seed), 6)
    part_splits = jax.random.split(jax.random.fold_in(splits[5], part), 6)
    queries = centred(part_splits[0], (SEQLEN, HEADS * HEAD_DIM), 1.0, 6.0, ((0, 4), (1, 4)))
    keys = draw_keys(jax.random.fold_in(jax.random.fold_in(splits[5], part), 71), part)
    values = centred(part_splits[2], (SEQLEN, HEADS * HEAD_DIM), 0.125, 0.75, ((0, 4), (1, 4)))
    out_grad = centred(part_splits[3], (SEQLEN, HEADS * HEAD_DIM), 0.125, 0.75, ((0, 4), (1, 4)))
    ridge = jnp.clip(jnp.exp(math.log(2.4) - 1.0986123 * jax.random.uniform(splits[4], (HEADS,), jnp.float32) ** block_scale(splits[4], (HEADS,), ((0, 4),), -0.2, 0.2)), 0.8, 2.4)
    return dict(queries=queries, keys=keys, values=values, out_grad=out_grad, ridge=ridge)


TINY_VALUE = 1e-30


def multiply(spec, left, right):
    return jnp.einsum(spec, left, right, precision=lax.Precision.HIGHEST)


def one_group(query_f, key_f, value_f, grad_f, ridge_f):
    width = query_f.shape[1]
    rows = jnp.arange(width)
    lower_mask = (rows[:, None] >= rows[None, :]).astype(jnp.float32)
    upper_mask = lower_mask.T
    key_gram = multiply('nchi,nchj->nhij', key_f, key_f)
    value_key = multiply('nchi,nchj->nhij', value_f, key_f)
    gram_start = jnp.cumsum(key_gram, 0) - key_gram
    memory_start = jnp.cumsum(value_key, 0) - value_key

    def apply_op(search):
        scores = multiply('nthd,nshd->nhts', search, key_f) * lower_mask
        return ridge_f * search + multiply('nhij,nchj->nchi', gram_start, search) + multiply('nhts,nshd->nthd', scores, key_f)

    def conjugate(target):
        solved = jnp.zeros_like(target)
        remain = target
        search = target
        norm_now = jnp.sum(remain * remain, -1, keepdims=True)
        for _ in range(CG_STEPS):
            image = apply_op(search)
            alpha = norm_now / (jnp.sum(search * image, -1, keepdims=True) + TINY_VALUE)
            solved = solved + alpha * search
            remain = remain - alpha * image
            norm_next = jnp.sum(remain * remain, -1, keepdims=True)
            search = remain + (norm_next / (norm_now + TINY_VALUE)) * search
            norm_now = norm_next
        return solved

    solved = conjugate(query_f)
    attend = multiply('nthd,nshd->nhts', solved, key_f) * lower_mask
    output = multiply('nhij,nchj->nchi', memory_start, solved) + multiply('nhts,nshd->nthd', attend, value_f)
    grad_scores = multiply('nthd,nshd->nhts', grad_f, value_f) * lower_mask
    pulled = multiply('nhij,nchi->nchj', memory_start, grad_f) + multiply('nhts,nshd->nthd', grad_scores, key_f)
    adjoint = conjugate(pulled)
    cross = multiply('nchi,nchj->nhij', adjoint, solved)
    pair_block = cross + jnp.transpose(cross, (0, 1, 3, 2))
    grad_block = multiply('nchi,nchj->nhij', grad_f, solved)
    pair_end = jnp.cumsum(pair_block[::-1], 0)[::-1] - pair_block
    grad_end = jnp.cumsum(grad_block[::-1], 0)[::-1] - grad_block
    key_solved = multiply('nihd,nthd->nhit', key_f, solved) * upper_mask
    key_adjoint = multiply('nihd,nthd->nhit', key_f, adjoint) * upper_mask
    value_scores = multiply('nihd,nthd->nhit', value_f, grad_f) * upper_mask
    key_out = -(multiply('nhij,nchj->nchi', pair_end, key_f) + multiply('nhit,nthd->nihd', key_solved, adjoint) + multiply('nhit,nthd->nihd', key_adjoint, solved)) + multiply('nhij,nchi->nchj', grad_end, value_f) + multiply('nhit,nthd->nihd', value_scores, solved)
    value_out = multiply('nhij,nchj->nchi', grad_end, key_f) + multiply('nhit,nthd->nihd', key_solved, grad_f)
    return output, adjoint, key_out, value_out


def reference(queries, keys, values, out_grad, ridge):
    blocks = SEQLEN // BLOCK

    def arrange(array):
        shaped = array.astype(jnp.float32).reshape(blocks, BLOCK, HEADS, HEAD_DIM)
        return jnp.transpose(shaped, (2, 0, 1, 3))[:, :, :, None, :]

    def per_head(members):
        return one_group(members[0], members[1], members[2], members[3], members[4])

    results = lax.map(per_head, (arrange(queries), arrange(keys), arrange(values), arrange(out_grad), ridge.astype(jnp.float32)))

    def restore(array):
        return jnp.transpose(array[:, :, :, 0, :], (1, 2, 0, 3)).reshape(SEQLEN, HEADS * HEAD_DIM)

    return (restore(results[0]), restore(results[1]), restore(results[2]), restore(results[3]))
```

```python
import functools

import jax
import jax.numpy as jnp
from jax import lax
from jax.experimental import pallas as pl
from jax.experimental.pallas import tpu as pltpu
from jax.sharding import PartitionSpec as P

D = 128
CG_STEPS = 4
TINY = 1e-30
F32 = jnp.float32
BF16 = jnp.bfloat16
MESH = pl.DeviceIdType.MESH


def split(a):
    hi = a.astype(BF16)
    lo = (a - hi.astype(F32)).astype(BF16)
    return hi, lo


def dot(a, b):
    return jnp.dot(a, b, preferred_element_type=F32)


def dot_t(a, b):
    return lax.dot_general(a, b, (((1,), (1,)), ((), ())), preferred_element_type=F32)


def colsum(a):
    return jnp.sum(a, axis=0, keepdims=True)


def kernel(n, heads, ridge_ref, q_ref, k_ref, v_ref, g_ref,
           out_ref, qg_ref, kg_ref, vg_ref,
           kt_ref, vt_ref, gt_ref, fown, fin, rown, rin,
           fsend, frecv, rsend, rrecv):
    z = lax.axis_index("seq")
    tokens = q_ref.shape[0]
    barrier = pltpu.get_barrier_semaphore()

    @pl.when(z > 0)
    def _():
        pl.semaphore_signal(barrier, inc=1, device_id={"seq": z - 1}, device_id_type=MESH)

    @pl.when(z < n - 1)
    def _():
        pl.semaphore_signal(barrier, inc=1, device_id={"seq": z + 1}, device_id_type=MESH)

    def cols(h):
        return pl.ds(pl.multiple_of(h * D, D), D)

    def fcopy(h, c):
        return pltpu.make_async_remote_copy(
            src_ref=fown.at[h, c], dst_ref=fin.at[h, c],
            send_sem=fsend.at[h, c], recv_sem=frecv.at[h, c],
            device_id={"seq": z + 1}, device_id_type=MESH)

    def rcopy(h, c):
        return pltpu.make_async_remote_copy(
            src_ref=rown.at[h, c], dst_ref=rin.at[h, c],
            send_sem=rsend.at[h, c], recv_sem=rrecv.at[h, c],
            device_id={"seq": z - 1}, device_id_type=MESH)

    @pl.when(z == 0)
    def _():
        fin[...] = jnp.zeros_like(fin)

    @pl.when(z == n - 1)
    def _():
        rin[...] = jnp.zeros_like(rin)

    def own(h, _):
        c = cols(h)
        k = k_ref[:, c]
        kt = k.astype(F32).T.astype(BF16)
        vt = v_ref[:, c].astype(F32).T.astype(BF16)
        kt_ref[h] = kt
        vt_ref[h] = vt
        gt_ref[h] = g_ref[:, c].astype(F32).T.astype(BF16)
        fown[h, 0] = dot(kt, k)
        fown[h, 1] = dot(vt, k)
        return 0

    lax.fori_loop(0, heads, own, 0)

    @pl.when((z > 0) & (z < n - 1))
    def _():
        pl.semaphore_wait(barrier, 2)

    @pl.when((z == 0) | (z == n - 1))
    def _():
        pl.semaphore_wait(barrier, 1)

    @pl.when(z == 0)
    def _():
        for h in range(heads):
            for c in range(2):
                fcopy(h, c).start()

    srow = lax.broadcasted_iota(jnp.int32, (tokens, tokens), 0)
    tcol = lax.broadcasted_iota(jnp.int32, (tokens, tokens), 1)
    mask = srow <= tcol

    def forward(h, _):
        for c in range(2):
            @pl.when(z > 0)
            def _():
                fcopy(h, c).wait_recv()

            @pl.when((z > 0) & (z < n - 1))
            def _():
                fown[h, c] = fown[h, c] + fin[h, c]
                fcopy(h, c).start()

        c = cols(h)
        k = k_ref[:, c]
        v = v_ref[:, c]
        kt = kt_ref[h]
        vt = vt_ref[h]
        gt = gt_ref[h]
        ridge = ridge_ref[h]
        kk = jnp.concatenate([k, k], axis=1)
        ghi, glo = split(fin[h, 0])
        gg = jnp.concatenate([ghi, ghi], axis=1)
        m = fin[h, 1]
        mhi, mlo = split(m)
        mm = jnp.concatenate([mhi, mhi], axis=1)
        mt = m.T
        mthi, mtlo = split(mt)

        vs = jnp.where(mask, dot(v, gt), 0.0)
        vh, vl = split(vs)
        pulled = dot(kt, vh) + dot(kt, vl) + dot(mthi, gt) + dot(mtlo, gt)
        query = q_ref[:, c].astype(F32).T

        def scores(ph, pp):
            return jnp.where(mask, dot(kk, pp), 0.0)

        state = []
        for b in (query, pulled):
            state.append([None, b, b, colsum(b * b)])
        for step in range(CG_STEPS):
            for one in state:
                s, r, p, rho = one
                ph, pl_ = split(p)
                pp = jnp.concatenate([ph, pl_], axis=0)
                sc = scores(ph, pp)
                gp = dot(gg, pp) + dot(glo, ph)
                if step < CG_STEPS - 1:
                    sh, sl = split(sc)
                    w = ridge * p + gp + dot(kt, sh) + dot(kt, sl)
                    alpha = rho / (colsum(p * w) + TINY)
                    s = alpha * p if s is None else s + alpha * p
                    r = r - alpha * w
                    rho2 = colsum(r * r)
                    p = r + (rho2 / (rho + TINY)) * p
                    one[:] = [s, r, p, rho2]
                else:
                    pw = colsum(p * (ridge * p + gp)) + colsum(sc * sc)
                    one[0] = s + (rho / (pw + TINY)) * p

        x, y = state[0][0], state[1][0]
        qg_ref[:, c] = y.T
        xh, xl = split(x)
        yh, yl = split(y)
        xx = jnp.concatenate([xh, xl], axis=0)
        yy = jnp.concatenate([yh, yl], axis=0)

        cross = dot_t(yh, xh) + dot_t(yl, xh) + dot_t(yh, xl)
        rown[h, 0] = cross + cross.T
        rown[h, 1] = dot_t(gt, xh) + dot_t(gt, xl)

        @pl.when(z == n - 1)
        def _():
            for c2 in range(2):
                rcopy(h, c2).start()

        ks = scores(xh, xx)
        ah, al = split(ks)
        out = dot(mm, xx) + dot(mlo, xh) + dot(vt, ah) + dot(vt, al)
        out_ref[:, c] = out.T
        ka = scores(yh, yy) - vs
        bh, bl = split(ka)
        kg_ref[:, c] = -(dot_t(ah, yh) + dot_t(al, yh) + dot_t(ah, yl)
                         + dot_t(bh, xh) + dot_t(bl, xh) + dot_t(bh, xl))
        vg_ref[:, c] = dot_t(ah, gt) + dot_t(al, gt)
        return 0

    lax.fori_loop(0, heads, forward, 0)

    def backward(h, _):
        for c in range(2):
            @pl.when(z < n - 1)
            def _():
                rcopy(h, c).wait_recv()

            @pl.when((z > 0) & (z < n - 1))
            def _():
                rown[h, c] = rown[h, c] + rin[h, c]
                rcopy(h, c).start()

        c = cols(h)
        k = k_ref[:, c]
        v = v_ref[:, c]
        ph, pl_ = split(rin[h, 0])
        qh, ql = split(rin[h, 1])
        kg_ref[:, c] = kg_ref[:, c] + (dot(v, qh) + dot(v, ql)) - (dot(k, ph) + dot(k, pl_))
        vg_ref[:, c] = vg_ref[:, c] + (dot_t(k, qh) + dot_t(k, ql))
        return 0

    lax.fori_loop(0, heads, backward, 0)

    for h in range(heads):
        for c in range(2):
            @pl.when(z < n - 1)
            def _():
                fcopy(h, c).wait_send()

            @pl.when(z > 0)
            def _():
                rcopy(h, c).wait_send()


def body(n, queries, keys, values, out_grad, ridge):
    tokens, width = queries.shape
    heads = width // D
    vm = pl.BlockSpec(memory_space=pltpu.VMEM)
    out = jax.ShapeDtypeStruct((tokens, width), F32)
    return pl.pallas_call(
        functools.partial(kernel, n, heads),
        out_shape=[out] * 4,
        in_specs=[pl.BlockSpec(memory_space=pltpu.SMEM)] + [vm] * 4,
        out_specs=[vm] * 4,
        scratch_shapes=[
            pltpu.VMEM((heads, D, tokens), BF16),
            pltpu.VMEM((heads, D, tokens), BF16),
            pltpu.VMEM((heads, D, tokens), BF16),
            pltpu.VMEM((heads, 2, D, D), F32),
            pltpu.VMEM((heads, 2, D, D), F32),
            pltpu.VMEM((heads, 2, D, D), F32),
            pltpu.VMEM((heads, 2, D, D), F32),
            pltpu.SemaphoreType.DMA((heads, 2)),
            pltpu.SemaphoreType.DMA((heads, 2)),
            pltpu.SemaphoreType.DMA((heads, 2)),
            pltpu.SemaphoreType.DMA((heads, 2)),
        ],
        compiler_params=pltpu.CompilerParams(
            collective_id=0, has_side_effects=True, vmem_limit_bytes=40 * 2**20),
        name="mesa",
    )(ridge, queries, keys, values, out_grad)


def solution(mesh):
    spec = P(("groups", "seq"), ("head", "sub"))
    return jax.shard_map(
        functools.partial(body, mesh.shape["seq"]), mesh=mesh,
        in_specs=(spec, spec, spec, spec, P(("head", "sub"))),
        out_specs=(spec, spec, spec, spec), check_vma=False)
```

```python
import functools

import jax
import jax.numpy as jnp
from jax import lax
from jax.experimental import pallas as pl
from jax.experimental.pallas import tpu as pltpu
from jax.sharding import PartitionSpec as P

D = 128
CG_STEPS = 4
LAG = 2
TINY = 1e-30
F32 = jnp.float32
BF16 = jnp.bfloat16
MESH = pl.DeviceIdType.MESH


def split(a):
    hi = a.astype(BF16)
    lo = (a - hi.astype(F32)).astype(BF16)
    return hi, lo


def dot(a, b):
    return jnp.dot(a, b, preferred_element_type=F32)


def dot_t(a, b):
    return lax.dot_general(a, b, (((1,), (1,)), ((), ())), preferred_element_type=F32)


def colsum(a):
    return jnp.sum(a, axis=0, keepdims=True)


H = D // 2
ROWS = H + 8 + D
CHUNKS = ((0, H + 8), (H + 8, H), (D + 8, H))


def iotas(shape):
    return lax.broadcasted_iota(jnp.int32, shape, 0), lax.broadcasted_iota(jnp.int32, shape, 1)


def pack(ref, a):
    r, c = iotas((H, D))
    top = a[:H]
    bot = pltpu.roll(a[H:], H, axis=1)
    ref[:H] = jnp.where((c < H) & (c > r), bot, top)
    ref[H:H + 8] = jnp.broadcast_to(colsum(jnp.where(c == r, bot, 0.0)), (8, D))


def unpack(ref):
    r, c = iotas((H, D))
    b = ref[:H]
    diag = ref[H:H + 8][:1]
    t = jnp.concatenate([b, jnp.zeros_like(b)], axis=0).T
    tl = t[:H]
    top = jnp.where((c < H) & (c > r), tl, b)
    low = jnp.where(c > r, b, jnp.where(c < r, tl, diag))
    bot = jnp.where(c < H, t[H:], pltpu.roll(low, H, axis=1))
    return jnp.concatenate([top, bot], axis=0)


def kernel(n, heads, ridge_ref, q_hbm, k_hbm, v_hbm, g_hbm,
           out_ref, qg_ref, kg_ref, vg_ref,
           q_ref, k_ref, v_ref, g_ref, load, kt_ref, vt_ref, fown, fin, rown, rin,
           fsend, frecv, rsend, rrecv):
    z = lax.axis_index("seq")
    tokens = q_ref.shape[0]
    loads = [pltpu.make_async_copy(a, b, load.at[i]) for i, (a, b) in enumerate(
        ((k_hbm, k_ref), (v_hbm, v_ref), (g_hbm, g_ref), (q_hbm, q_ref)))]
    for one in loads:
        one.start()
    barrier = pltpu.get_barrier_semaphore()

    @pl.when(z > 0)
    def _():
        pl.semaphore_signal(barrier, inc=1, device_id={"seq": z - 1}, device_id_type=MESH)

    @pl.when(z < n - 1)
    def _():
        pl.semaphore_signal(barrier, inc=1, device_id={"seq": z + 1}, device_id_type=MESH)

    def cols(h):
        return pl.ds(pl.multiple_of(h * D, D), D)

    def part(c):
        return pl.ds(*CHUNKS[c])

    def fcopy(h, c):
        return pltpu.make_async_remote_copy(
            src_ref=fown.at[h, part(c)], dst_ref=fin.at[h, part(c)],
            send_sem=fsend.at[h, c], recv_sem=frecv.at[h, c],
            device_id={"seq": z + 1}, device_id_type=MESH)

    def rcopy(h, c):
        return pltpu.make_async_remote_copy(
            src_ref=rown.at[h, part(c)], dst_ref=rin.at[h, part(c)],
            send_sem=rsend.at[h, c], recv_sem=rrecv.at[h, c],
            device_id={"seq": z - 1}, device_id_type=MESH)

    @pl.when(z == 0)
    def _():
        fin[...] = jnp.zeros_like(fin)

    @pl.when(z == n - 1)
    def _():
        rin[...] = jnp.zeros_like(rin)

    def own(h, _):
        c = cols(h)
        k = k_ref[:, c]
        kt = k.astype(F32).T.astype(BF16)
        vt = v_ref[:, c].astype(F32).T.astype(BF16)
        kt_ref[h] = kt
        vt_ref[h] = vt
        pack(fown.at[h], dot(kt, k))
        fown[h, H + 8:] = dot(vt, k)
        return 0

    loads[0].wait()
    loads[1].wait()
    lax.fori_loop(0, heads, own, 0)

    @pl.when((z > 0) & (z < n - 1))
    def _():
        pl.semaphore_wait(barrier, 2)

    @pl.when((z == 0) | (z == n - 1))
    def _():
        pl.semaphore_wait(barrier, 1)

    @pl.when(z == 0)
    def _():
        for h in range(heads):
            for c in range(3):
                fcopy(h, c).start()

    srow = lax.broadcasted_iota(jnp.int32, (tokens, tokens), 0)
    tcol = lax.broadcasted_iota(jnp.int32, (tokens, tokens), 1)
    mask = srow <= tcol

    loads[2].wait()
    loads[3].wait()

    def backward(h, _):
        for c in range(3):
            @pl.when(z < n - 1)
            def _():
                rcopy(h, c).wait_recv()

            @pl.when((z > 0) & (z < n - 1))
            def _():
                rown[h, part(c)] = rown[h, part(c)] + rin[h, part(c)]
                rcopy(h, c).start()

        c = cols(h)
        k = k_ref[:, c]
        v = v_ref[:, c]
        ph, pl_ = split(unpack(rin.at[h]))
        qh, ql = split(rin[h, H + 8:])
        kg_ref[:, c] = kg_ref[:, c] + (dot(v, qh) + dot(v, ql)) - (dot(k, ph) + dot(k, pl_))
        vg_ref[:, c] = vg_ref[:, c] + (dot_t(k, qh) + dot_t(k, ql))
        return 0

    def forward(h, _):
        for c in range(3):
            @pl.when(z > 0)
            def _():
                fcopy(h, c).wait_recv()

            @pl.when((z > 0) & (z < n - 1))
            def _():
                fown[h, part(c)] = fown[h, part(c)] + fin[h, part(c)]
                fcopy(h, c).start()

        c = cols(h)
        k = k_ref[:, c]
        v = v_ref[:, c]
        kt = kt_ref[h]
        vt = vt_ref[h]
        gt = g_ref[:, c].astype(F32).T.astype(BF16)
        ridge = ridge_ref[h]
        kk = jnp.concatenate([k, k], axis=1)
        ghi, glo = split(unpack(fin.at[h]))
        gg = jnp.concatenate([ghi, ghi], axis=1)
        m = fin[h, H + 8:]
        mhi, mlo = split(m)
        mm = jnp.concatenate([mhi, mhi], axis=1)
        mt = m.T
        mthi, mtlo = split(mt)

        vs = jnp.where(mask, dot(v, gt), 0.0)
        vh, vl = split(vs)
        pulled = dot(kt, vh) + dot(kt, vl) + dot(mthi, gt) + dot(mtlo, gt)
        query = q_ref[:, c].astype(F32).T

        def scores(ph, pp):
            return jnp.where(mask, dot(kk, pp), 0.0)

        state = []
        for b in (query, pulled):
            state.append([None, b, b, colsum(b * b)])
        for step in range(CG_STEPS):
            for one in state:
                s, r, p, rho = one
                ph, pl_ = split(p)
                pp = jnp.concatenate([ph, pl_], axis=0)
                sc = scores(ph, pp)
                gp = dot(gg, pp) + dot(glo, ph)
                if step < CG_STEPS - 1:
                    sh, sl = split(sc)
                    w = ridge * p + gp + dot(kt, sh) + dot(kt, sl)
                    alpha = rho / (colsum(p * w) + TINY)
                    s = alpha * p if s is None else s + alpha * p
                    r = r - alpha * w
                    rho2 = colsum(r * r)
                    p = r + (rho2 / (rho + TINY)) * p
                    one[:] = [s, r, p, rho2]
                else:
                    pw = colsum(p * (ridge * p + gp)) + colsum(sc * sc)
                    one[0] = s + (rho / (pw + TINY)) * p

        x, y = state[0][0], state[1][0]
        qg_ref[:, c] = y.T
        xh, xl = split(x)
        yh, yl = split(y)
        xx = jnp.concatenate([xh, xl], axis=0)
        yy = jnp.concatenate([yh, yl], axis=0)

        cross = dot_t(yh, xh) + dot_t(yl, xh) + dot_t(yh, xl)
        pack(rown.at[h], cross + cross.T)
        rown[h, H + 8:] = dot_t(gt, xh) + dot_t(gt, xl)

        @pl.when(z == n - 1)
        def _():
            for c2 in range(3):
                rcopy(h, c2).start()

        ks = scores(xh, xx)
        ah, al = split(ks)
        out = dot(mm, xx) + dot(mlo, xh) + dot(vt, ah) + dot(vt, al)
        out_ref[:, c] = out.T
        ka = scores(yh, yy) - vs
        bh, bl = split(ka)
        kg_ref[:, c] = -(dot_t(ah, yh) + dot_t(al, yh) + dot_t(ah, yl)
                         + dot_t(bh, xh) + dot_t(bl, xh) + dot_t(bh, xl))
        vg_ref[:, c] = dot_t(ah, gt) + dot_t(al, gt)

        @pl.when((z == n - 2) & (h >= LAG))
        def _():
            backward(h - LAG, 0)

        return 0

    lax.fori_loop(0, heads, forward, 0)

    lax.fori_loop(jnp.where(z == n - 2, max(heads - LAG, 0), 0), heads, backward, 0)

    for h in range(heads):
        for c in range(3):
            @pl.when(z < n - 1)
            def _():
                fcopy(h, c).wait_send()

            @pl.when(z > 0)
            def _():
                rcopy(h, c).wait_send()


def store(*refs):
    sems = refs[8]
    copies = [pltpu.make_async_copy(refs[i], refs[i + 4], sems.at[i]) for i in range(4)]
    for one in copies:
        one.start()
    for one in copies:
        one.wait()


def body(n, queries, keys, values, out_grad, ridge):
    tokens, width = queries.shape
    heads = width // D
    hbm = pl.BlockSpec(memory_space=pltpu.HBM)
    vm = pl.BlockSpec(memory_space=pltpu.VMEM)
    out = jax.ShapeDtypeStruct((tokens, width), F32)
    parts = pl.pallas_call(
        functools.partial(kernel, n, heads),
        out_shape=[out] * 4,
        in_specs=[pl.BlockSpec(memory_space=pltpu.SMEM)] + [hbm] * 4,
        out_specs=[vm] * 4,
        scratch_shapes=[
            *[pltpu.VMEM((tokens, width), BF16)] * 4,
            pltpu.SemaphoreType.DMA((4,)),
            *[pltpu.VMEM((heads, D, tokens), BF16)] * 2,
            *[pltpu.VMEM((heads, ROWS, D), F32)] * 4,
            *[pltpu.SemaphoreType.DMA((heads, 3))] * 4,
        ],
        compiler_params=pltpu.CompilerParams(
            collective_id=0, has_side_effects=True, vmem_limit_bytes=24 * 2**20),
        name="mesa",
    )(ridge, queries, keys, values, out_grad)
    return pl.pallas_call(
        store, out_shape=[out] * 4, in_specs=[vm] * 4, out_specs=[hbm] * 4,
        scratch_shapes=[pltpu.SemaphoreType.DMA((4,))], name="store",
    )(*parts)


def solution(mesh):
    spec = P(("groups", "seq"), ("head", "sub"))
    return jax.shard_map(
        functools.partial(body, mesh.shape["seq"]), mesh=mesh,
        in_specs=(spec, spec, spec, spec, P(("head", "sub"))),
        out_specs=(spec, spec, spec, spec), check_vma=False)
```

```python
import functools

import jax
import jax.numpy as jnp
from jax import lax
from jax.experimental import pallas as pl
from jax.experimental.pallas import tpu as pltpu
from jax.sharding import PartitionSpec as P

D = 128
CG_STEPS = 4
LAG = 2
TINY = 1e-30
F32 = jnp.float32
BF16 = jnp.bfloat16
MESH = pl.DeviceIdType.MESH


def split(a):
    hi = a.astype(BF16)
    lo = (a - hi.astype(F32)).astype(BF16)
    return hi, lo


def dot(a, b):
    return jnp.dot(a, b, preferred_element_type=F32)


def dot_t(a, b):
    return lax.dot_general(a, b, (((1,), (1,)), ((), ())), preferred_element_type=F32)


def colsum(a):
    return jnp.sum(a, axis=0, keepdims=True)


H = D // 2
ROWS = H + 8 + D
CHUNKS = ((0, H + 8), (H + 8, H), (D + 8, H))


def iotas(shape):
    return lax.broadcasted_iota(jnp.int32, shape, 0), lax.broadcasted_iota(jnp.int32, shape, 1)


def pack(ref, a):
    r, c = iotas((H, D))
    top = a[:H]
    bot = pltpu.roll(a[H:], H, axis=1)
    ref[:H] = jnp.where((c < H) & (c > r), bot, top)
    ref[H:H + 8] = jnp.broadcast_to(colsum(jnp.where(c == r, bot, 0.0)), (8, D))


def unpack(ref):
    r, c = iotas((H, D))
    b = ref[:H]
    diag = ref[H:H + 8][:1]
    t = jnp.concatenate([b, jnp.zeros_like(b)], axis=0).T
    tl = t[:H]
    top = jnp.where((c < H) & (c > r), tl, b)
    low = jnp.where(c > r, b, jnp.where(c < r, tl, diag))
    bot = jnp.where(c < H, t[H:], pltpu.roll(low, H, axis=1))
    return jnp.concatenate([top, bot], axis=0)


def kernel(n, heads, ridge_ref, q_hbm, k_hbm, v_hbm, g_hbm,
           out_hbm, qg_hbm, kg_hbm, vg_hbm,
           out_ref, qg_ref, kg_ref, vg_ref, stored,
           q_ref, k_ref, v_ref, g_ref, load, kt_ref, vt_ref, fown, fin, rown, rin,
           fsend, frecv, rsend, rrecv):
    z = lax.axis_index("seq")
    tokens = q_ref.shape[0]
    loads = [pltpu.make_async_copy(a, b, load.at[i]) for i, (a, b) in enumerate(
        ((k_hbm, k_ref), (v_hbm, v_ref), (g_hbm, g_ref), (q_hbm, q_ref)))]
    for one in loads:
        one.start()
    barrier = pltpu.get_barrier_semaphore()

    @pl.when(z > 0)
    def _():
        pl.semaphore_signal(barrier, inc=1, device_id={"seq": z - 1}, device_id_type=MESH)

    @pl.when(z < n - 1)
    def _():
        pl.semaphore_signal(barrier, inc=1, device_id={"seq": z + 1}, device_id_type=MESH)

    def cols(h):
        return pl.ds(pl.multiple_of(h * D, D), D)

    def save(i, h):
        a, b = ((out_ref, out_hbm), (qg_ref, qg_hbm), (kg_ref, kg_hbm), (vg_ref, vg_hbm))[i]
        return pltpu.make_async_copy(a.at[:, cols(h)], b.at[:, cols(h)], stored.at[i, h])

    def part(c):
        return pl.ds(*CHUNKS[c])

    def fcopy(h, c):
        return pltpu.make_async_remote_copy(
            src_ref=fown.at[h, part(c)], dst_ref=fin.at[h, part(c)],
            send_sem=fsend.at[h, c], recv_sem=frecv.at[h, c],
            device_id={"seq": z + 1}, device_id_type=MESH)

    def rcopy(h, c):
        return pltpu.make_async_remote_copy(
            src_ref=rown.at[h, part(c)], dst_ref=rin.at[h, part(c)],
            send_sem=rsend.at[h, c], recv_sem=rrecv.at[h, c],
            device_id={"seq": z - 1}, device_id_type=MESH)

    @pl.when(z == 0)
    def _():
        fin[...] = jnp.zeros_like(fin)

    @pl.when(z == n - 1)
    def _():
        rin[...] = jnp.zeros_like(rin)

    def own(h, _):
        c = cols(h)
        k = k_ref[:, c]
        kt = k.astype(F32).T.astype(BF16)
        vt = v_ref[:, c].astype(F32).T.astype(BF16)
        kt_ref[h] = kt
        vt_ref[h] = vt
        pack(fown.at[h], dot(kt, k))
        fown[h, H + 8:] = dot(vt, k)
        return 0

    loads[0].wait()
    loads[1].wait()
    lax.fori_loop(0, heads, own, 0)

    @pl.when((z > 0) & (z < n - 1))
    def _():
        pl.semaphore_wait(barrier, 2)

    @pl.when((z == 0) | (z == n - 1))
    def _():
        pl.semaphore_wait(barrier, 1)

    @pl.when(z == 0)
    def _():
        for h in range(heads):
            for c in range(3):
                fcopy(h, c).start()

    srow = lax.broadcasted_iota(jnp.int32, (tokens, tokens), 0)
    tcol = lax.broadcasted_iota(jnp.int32, (tokens, tokens), 1)
    mask = srow <= tcol

    loads[2].wait()
    loads[3].wait()

    def backward(h, _):
        for c in range(3):
            @pl.when(z < n - 1)
            def _():
                rcopy(h, c).wait_recv()

            @pl.when((z > 0) & (z < n - 1))
            def _():
                rown[h, part(c)] = rown[h, part(c)] + rin[h, part(c)]
                rcopy(h, c).start()

        c = cols(h)
        k = k_ref[:, c]
        v = v_ref[:, c]
        ph, pl_ = split(unpack(rin.at[h]))
        qh, ql = split(rin[h, H + 8:])
        kg_ref[:, c] = kg_ref[:, c] + (dot(v, qh) + dot(v, ql)) - (dot(k, ph) + dot(k, pl_))
        vg_ref[:, c] = vg_ref[:, c] + (dot_t(k, qh) + dot_t(k, ql))
        save(2, h).start()
        save(3, h).start()
        return 0

    def forward(h, _):
        for c in range(3):
            @pl.when(z > 0)
            def _():
                fcopy(h, c).wait_recv()

            @pl.when((z > 0) & (z < n - 1))
            def _():
                fown[h, part(c)] = fown[h, part(c)] + fin[h, part(c)]
                fcopy(h, c).start()

        c = cols(h)
        k = k_ref[:, c]
        v = v_ref[:, c]
        kt = kt_ref[h]
        vt = vt_ref[h]
        gt = g_ref[:, c].astype(F32).T.astype(BF16)
        ridge = ridge_ref[h]
        kk = jnp.concatenate([k, k], axis=1)
        ghi, glo = split(unpack(fin.at[h]))
        gg = jnp.concatenate([ghi, ghi], axis=1)
        m = fin[h, H + 8:]
        mhi, mlo = split(m)
        mm = jnp.concatenate([mhi, mhi], axis=1)
        mt = m.T
        mthi, mtlo = split(mt)

        vs = jnp.where(mask, dot(v, gt), 0.0)
        vh, vl = split(vs)
        pulled = dot(kt, vh) + dot(kt, vl) + dot(mthi, gt) + dot(mtlo, gt)
        query = q_ref[:, c].astype(F32).T

        def scores(ph, pp):
            return jnp.where(mask, dot(kk, pp), 0.0)

        state = []
        for b in (query, pulled):
            state.append([None, b, b, colsum(b * b)])
        for step in range(CG_STEPS):
            for one in state:
                s, r, p, rho = one
                ph, pl_ = split(p)
                pp = jnp.concatenate([ph, pl_], axis=0)
                sc = scores(ph, pp)
                gp = dot(gg, pp) + dot(glo, ph)
                if step < CG_STEPS - 1:
                    sh, sl = split(sc)
                    w = ridge * p + gp + dot(kt, sh) + dot(kt, sl)
                    alpha = rho / (colsum(p * w) + TINY)
                    s = alpha * p if s is None else s + alpha * p
                    r = r - alpha * w
                    rho2 = colsum(r * r)
                    p = r + (rho2 / (rho + TINY)) * p
                    one[:] = [s, r, p, rho2]
                else:
                    pw = colsum(p * (ridge * p + gp)) + colsum(sc * sc)
                    one[0] = s + (rho / (pw + TINY)) * p

        x, y = state[0][0], state[1][0]
        qg_ref[:, c] = y.T
        save(1, h).start()
        xh, xl = split(x)
        yh, yl = split(y)
        xx = jnp.concatenate([xh, xl], axis=0)
        yy = jnp.concatenate([yh, yl], axis=0)

        cross = dot_t(yh, xh) + dot_t(yl, xh) + dot_t(yh, xl)
        pack(rown.at[h], cross + cross.T)
        rown[h, H + 8:] = dot_t(gt, xh) + dot_t(gt, xl)

        @pl.when(z == n - 1)
        def _():
            for c2 in range(3):
                rcopy(h, c2).start()

        ks = scores(xh, xx)
        ah, al = split(ks)
        out = dot(mm, xx) + dot(mlo, xh) + dot(vt, ah) + dot(vt, al)
        out_ref[:, c] = out.T
        save(0, h).start()
        ka = scores(yh, yy) - vs
        bh, bl = split(ka)
        kg_ref[:, c] = -(dot_t(ah, yh) + dot_t(al, yh) + dot_t(ah, yl)
                         + dot_t(bh, xh) + dot_t(bl, xh) + dot_t(bh, xl))
        vg_ref[:, c] = dot_t(ah, gt) + dot_t(al, gt)

        @pl.when((z == n - 2) & (h >= LAG))
        def _():
            backward(h - LAG, 0)

        return 0

    lax.fori_loop(0, heads, forward, 0)

    lax.fori_loop(jnp.where(z == n - 2, max(heads - LAG, 0), 0), heads, backward, 0)

    for h in range(heads):
        for i in range(4):
            save(i, h).wait()
        for c in range(3):
            @pl.when(z < n - 1)
            def _():
                fcopy(h, c).wait_send()

            @pl.when(z > 0)
            def _():
                rcopy(h, c).wait_send()


def store(*refs):
    sems = refs[8]
    copies = [pltpu.make_async_copy(refs[i], refs[i + 4], sems.at[i]) for i in range(4)]
    for one in copies:
        one.start()
    for one in copies:
        one.wait()


def body(n, queries, keys, values, out_grad, ridge):
    tokens, width = queries.shape
    heads = width // D
    hbm = pl.BlockSpec(memory_space=pl.ANY)
    out = jax.ShapeDtypeStruct((tokens, width), F32)
    parts = pl.pallas_call(
        functools.partial(kernel, n, heads),
        out_shape=[out] * 4,
        in_specs=[pl.BlockSpec(memory_space=pltpu.SMEM)] + [hbm] * 4,
        out_specs=[hbm] * 4,
        scratch_shapes=[
            *[pltpu.VMEM((tokens, width), F32)] * 4,
            pltpu.SemaphoreType.DMA((4, heads)),
            *[pltpu.VMEM((tokens, width), BF16)] * 4,
            pltpu.SemaphoreType.DMA((4,)),
            *[pltpu.VMEM((heads, D, tokens), BF16)] * 2,
            *[pltpu.VMEM((heads, ROWS, D), F32)] * 4,
            *[pltpu.SemaphoreType.DMA((heads, 3))] * 4,
        ],
        compiler_params=pltpu.CompilerParams(
            collective_id=0, has_side_effects=True, vmem_limit_bytes=56 * 2**20),
        name="mesa",
    )(ridge, queries, keys, values, out_grad)
    return pl.pallas_call(
        store, out_shape=[out] * 4, in_specs=[hbm] * 4, out_specs=[hbm] * 4,
        scratch_shapes=[pltpu.SemaphoreType.DMA((4,))], name="store",
    )(*parts)


def solution(mesh):
    spec = P(("groups", "seq"), ("head", "sub"))
    return jax.shard_map(
        functools.partial(body, mesh.shape["seq"]), mesh=mesh,
        in_specs=(spec, spec, spec, spec, P(("head", "sub"))),
        out_specs=(spec, spec, spec, spec), check_vma=False)
```

```python
import functools

import jax
import jax.numpy as jnp
from jax import lax
from jax.experimental import pallas as pl
from jax.experimental.pallas import tpu as pltpu
from jax.sharding import PartitionSpec as P

D = 128
CG_STEPS = 4
LAG = 2
TINY = 1e-30
F32 = jnp.float32
BF16 = jnp.bfloat16
MESH = pl.DeviceIdType.MESH


def split(a):
    hi = a.astype(BF16)
    lo = (a - hi.astype(F32)).astype(BF16)
    return hi, lo


def dot(a, b):
    return jnp.dot(a, b, preferred_element_type=F32)


def dot_t(a, b):
    return lax.dot_general(a, b, (((1,), (1,)), ((), ())), preferred_element_type=F32)


def colsum(a):
    return jnp.sum(a, axis=0, keepdims=True)


H = D // 2
ROWS = H + 8 + D
CHUNKS = ((0, H + 8), (H + 8, H), (D + 8, H))


def iotas(shape):
    return lax.broadcasted_iota(jnp.int32, shape, 0), lax.broadcasted_iota(jnp.int32, shape, 1)


def pack(ref, a):
    r, c = iotas((H, D))
    top = a[:H]
    bot = pltpu.roll(a[H:], H, axis=1)
    ref[:H] = jnp.where((c < H) & (c > r), bot, top)
    ref[H:H + 8] = jnp.broadcast_to(colsum(jnp.where(c == r, bot, 0.0)), (8, D))


def unpack(ref):
    r, c = iotas((H, D))
    b = ref[:H]
    diag = ref[H:H + 8][:1]
    t = jnp.concatenate([b, jnp.zeros_like(b)], axis=0).T
    tl = t[:H]
    top = jnp.where((c < H) & (c > r), tl, b)
    low = jnp.where(c > r, b, jnp.where(c < r, tl, diag))
    bot = jnp.where(c < H, t[H:], pltpu.roll(low, H, axis=1))
    return jnp.concatenate([top, bot], axis=0)


def kernel(n, heads, ridge_ref, q_hbm, k_hbm, v_hbm, g_hbm,
           out_hbm, qg_hbm, kg_hbm, vg_hbm,
           out_ref, qg_ref, kg_ref, vg_ref, stored,
           q_ref, k_ref, v_ref, g_ref, load, kt_ref, vt_ref, fown, fin, rown, rin,
           fsend, frecv, rsend, rrecv):
    z = lax.axis_index("seq")
    tokens = q_ref.shape[0]
    loads = [pltpu.make_async_copy(a, b, load.at[i]) for i, (a, b) in enumerate(
        ((k_hbm, k_ref), (v_hbm, v_ref), (g_hbm, g_ref), (q_hbm, q_ref)))]
    for one in loads:
        one.start()
    barrier = pltpu.get_barrier_semaphore()

    @pl.when(z > 0)
    def _():
        pl.semaphore_signal(barrier, inc=1, device_id={"seq": z - 1}, device_id_type=MESH)

    @pl.when(z < n - 1)
    def _():
        pl.semaphore_signal(barrier, inc=1, device_id={"seq": z + 1}, device_id_type=MESH)

    def cols(h):
        return pl.ds(pl.multiple_of(h * D, D), D)

    def save(i, h):
        a, b = ((out_ref, out_hbm), (qg_ref, qg_hbm), (kg_ref, kg_hbm), (vg_ref, vg_hbm))[i]
        return pltpu.make_async_copy(a.at[:, cols(h)], b.at[:, cols(h)], stored.at[i, h])

    def part(c):
        return pl.ds(*CHUNKS[c])

    def fcopy(h, c):
        return pltpu.make_async_remote_copy(
            src_ref=fown.at[h, part(c)], dst_ref=fin.at[h, part(c)],
            send_sem=fsend.at[h, c], recv_sem=frecv.at[h, c],
            device_id={"seq": z + 1}, device_id_type=MESH)

    def rcopy(h, c):
        return pltpu.make_async_remote_copy(
            src_ref=rown.at[h, part(c)], dst_ref=rin.at[h, part(c)],
            send_sem=rsend.at[h, c], recv_sem=rrecv.at[h, c],
            device_id={"seq": z - 1}, device_id_type=MESH)

    @pl.when(z == 0)
    def _():
        fin[...] = jnp.zeros_like(fin)

    @pl.when(z == n - 1)
    def _():
        rin[...] = jnp.zeros_like(rin)

    def own(h, _):
        c = cols(h)
        k = k_ref[:, c]
        kt = k.astype(F32).T.astype(BF16)
        vt = v_ref[:, c].astype(F32).T.astype(BF16)
        kt_ref[h] = kt
        vt_ref[h] = vt
        pack(fown.at[h], dot(kt, k))
        fown[h, H + 8:] = dot(vt, k)
        return 0

    loads[0].wait()
    loads[1].wait()
    lax.fori_loop(0, heads, own, 0)

    @pl.when((z > 0) & (z < n - 1))
    def _():
        pl.semaphore_wait(barrier, 2)

    @pl.when((z == 0) | (z == n - 1))
    def _():
        pl.semaphore_wait(barrier, 1)

    @pl.when(z == 0)
    def _():
        for h in range(heads):
            for c in range(3):
                fcopy(h, c).start()

    srow = lax.broadcasted_iota(jnp.int32, (tokens, tokens), 0)
    tcol = lax.broadcasted_iota(jnp.int32, (tokens, tokens), 1)
    mask = srow <= tcol

    loads[2].wait()
    loads[3].wait()

    def backward(h, _):
        for c in range(3):
            @pl.when(z < n - 1)
            def _():
                rcopy(h, c).wait_recv()

            @pl.when((z > 0) & (z < n - 1))
            def _():
                rown[h, part(c)] = rown[h, part(c)] + rin[h, part(c)]
                rcopy(h, c).start()

        c = cols(h)
        k = k_ref[:, c]
        v = v_ref[:, c]
        ph, pl_ = split(unpack(rin.at[h]))
        qh, ql = split(rin[h, H + 8:])
        kg_ref[:, c] = kg_ref[:, c] + (dot(v, qh) + dot(v, ql)) - (dot(k, ph) + dot(k, pl_))
        vg_ref[:, c] = vg_ref[:, c] + (dot_t(k, qh) + dot_t(k, ql))
        save(2, h).start()
        save(3, h).start()
        return 0

    def forward(h, _):
        for c in range(3):
            @pl.when(z > 0)
            def _():
                fcopy(h, c).wait_recv()

            @pl.when((z > 0) & (z < n - 1))
            def _():
                fown[h, part(c)] = fown[h, part(c)] + fin[h, part(c)]
                fcopy(h, c).start()

        c = cols(h)
        k = k_ref[:, c]
        v = v_ref[:, c]
        kt = kt_ref[h]
        vt = vt_ref[h]
        gt = g_ref[:, c].astype(F32).T.astype(BF16)
        ridge = ridge_ref[h]
        kk = jnp.concatenate([k, k], axis=1)
        ghi, glo = split(unpack(fin.at[h]))
        gg = jnp.concatenate([ghi, ghi], axis=1)
        m = fin[h, H + 8:]
        mhi, mlo = split(m)
        mm = jnp.concatenate([mhi, mhi], axis=1)
        mt = m.T
        mthi, mtlo = split(mt)

        vs = jnp.where(mask, dot(v, gt), 0.0)
        vh, vl = split(vs)
        pulled = dot(kt, vh) + dot(kt, vl) + dot(mthi, gt) + dot(mtlo, gt)
        query = q_ref[:, c].astype(F32).T

        def scores(ph, pp):
            return jnp.where(mask, dot(kk, pp), 0.0)

        state = []
        for b in (query, pulled):
            state.append([None, b, b, colsum(b * b)])
        for step in range(CG_STEPS):
            for one in state:
                s, r, p, rho = one
                ph, pl_ = split(p)
                pp = jnp.concatenate([ph, pl_], axis=0)
                sc = scores(ph, pp)
                gp = dot(gg, pp) + dot(glo, ph)
                if step < CG_STEPS - 1:
                    sh, sl = split(sc)
                    w = ridge * p + gp + dot(kt, sh) + dot(kt, sl)
                    alpha = rho / (colsum(p * w) + TINY)
                    s = alpha * p if s is None else s + alpha * p
                    r = r - alpha * w
                    rho2 = colsum(r * r)
                    p = r + (rho2 / (rho + TINY)) * p
                    one[:] = [s, r, p, rho2]
                else:
                    pw = colsum(p * (ridge * p + gp)) + colsum(sc * sc)
                    one[0] = s + (rho / (pw + TINY)) * p

        x, y = state[0][0], state[1][0]
        qg_ref[:, c] = y.T
        save(1, h).start()
        xh, xl = split(x)
        yh, yl = split(y)
        xx = jnp.concatenate([xh, xl], axis=0)
        yy = jnp.concatenate([yh, yl], axis=0)

        cross = dot_t(yh, xh) + dot_t(yl, xh) + dot_t(yh, xl)
        pack(rown.at[h], cross + cross.T)
        rown[h, H + 8:] = dot_t(gt, xh) + dot_t(gt, xl)

        @pl.when(z == n - 1)
        def _():
            for c2 in range(3):
                rcopy(h, c2).start()

        ks = scores(xh, xx)
        ah, al = split(ks)
        out = dot(mm, xx) + dot(mlo, xh) + dot(vt, ah) + dot(vt, al)
        out_ref[:, c] = out.T
        save(0, h).start()
        ka = scores(yh, yy) - vs
        bh, bl = split(ka)
        kg_ref[:, c] = -(dot_t(ah, yh) + dot_t(al, yh) + dot_t(ah, yl)
                         + dot_t(bh, xh) + dot_t(bl, xh) + dot_t(bh, xl))
        vg_ref[:, c] = dot_t(ah, gt) + dot_t(al, gt)

        @pl.when((z == n - 2) & (h >= LAG))
        def _():
            backward(h - LAG, 0)

        return 0

    lax.fori_loop(0, heads, forward, 0)

    lax.fori_loop(jnp.where(z == n - 2, max(heads - LAG, 0), 0), heads, backward, 0)

    for h in range(heads):
        for i in range(4):
            save(i, h).wait()
        for c in range(3):
            @pl.when(z < n - 1)
            def _():
                fcopy(h, c).wait_send()

            @pl.when(z > 0)
            def _():
                rcopy(h, c).wait_send()


def store(*refs):
    sems = refs[8]
    copies = [pltpu.make_async_copy(refs[i], refs[i + 4], sems.at[i]) for i in range(4)]
    for one in copies:
        one.start()
    for one in copies:
        one.wait()


def body(n, queries, keys, values, out_grad, ridge):
    tokens, width = queries.shape
    heads = width // D
    hbm = pl.BlockSpec(memory_space=pl.ANY)
    vm = pl.BlockSpec(memory_space=pltpu.VMEM)
    out = jax.ShapeDtypeStruct((tokens, width), F32)
    parts = pl.pallas_call(
        functools.partial(kernel, n, heads),
        out_shape=[out] * 4,
        in_specs=[pl.BlockSpec(memory_space=pltpu.SMEM)] + [hbm] * 4,
        out_specs=[hbm] * 4,
        scratch_shapes=[
            *[pltpu.VMEM((tokens, width), F32)] * 4,
            pltpu.SemaphoreType.DMA((4, heads)),
            *[pltpu.VMEM((tokens, width), BF16)] * 4,
            pltpu.SemaphoreType.DMA((4,)),
            *[pltpu.VMEM((heads, D, tokens), BF16)] * 2,
            *[pltpu.VMEM((heads, ROWS, D), F32)] * 4,
            *[pltpu.SemaphoreType.DMA((heads, 3))] * 4,
        ],
        compiler_params=pltpu.CompilerParams(
            collective_id=0, has_side_effects=True, vmem_limit_bytes=56 * 2**20),
        name="mesa",
    )(ridge, queries, keys, values, out_grad)
    return pl.pallas_call(
        store, out_shape=[out] * 4, in_specs=[vm] * 4, out_specs=[hbm] * 4,
        scratch_shapes=[pltpu.SemaphoreType.DMA((4,))], name="store",
    )(*parts)


def solution(mesh):
    spec = P(("groups", "seq"), ("head", "sub"))
    return jax.shard_map(
        functools.partial(body, mesh.shape["seq"]), mesh=mesh,
        in_specs=(spec, spec, spec, spec, P(("head", "sub"))),
        out_specs=(spec, spec, spec, spec), check_vma=False)
```
